512 devices in a mesh: comp: 8 (over x, y_hi), row: 64 (over z, y_lo, core).
Axes of the slice: x: 4, y: 8 (y_hi: 2, y_lo: 4; y = y_hi * 4 + y_lo), z: 8, core: 2. Of those that a mesh axis runs over, the one named last changes fastest.
Arguments:
- features: float32 [8, 16, 32768], P('comp', None, 'row'), may hold values from -6 to 6
- lengthscale: float32 [8, 16], P('comp'), may hold values from 1 to 3
- amplitude: float32 [8], P('comp'), may hold values from 0.5 to 2
- noise: float32 [1], replicated, may hold values from 0.5 to 2
- solution: float32 [128, 32768], P(None, 'row'), may hold values from -6 to 6
- residual: float32 [128, 32768], P(None, 'row'), may hold values from -12 to 12
- direction: float32 [128, 32768], P(None, 'row'), may hold values from -6 to 6
Outputs:
- new_solution: float32 [128, 32768], P(None, 'row')
- new_residual: float32 [128, 32768], P(None, 'row')
- new_direction: float32 [128, 32768], P(None, 'row')
The draws below stay inside these ranges and needn't reach their ends.
All inputs are finite; a program needn't handle non-finite values.
Results may differ from the reference program's by a relative error of at most 0.017.
Values may be sent and summed in bfloat16 or wider, within the bound.
No kernel may reach another device: no remote copies, remote signals or barrier semaphores. Data moves between devices by JAX's collectives and lax.ppermute only.
A program may use at most 64 MiB of HBM per device.

```python
import math
import jax
import jax.numpy as jnp
from jax import lax

COMPS = 8
FEAT = 16
PROBES = 128
POINTS = 32768


def draw_residual(key, part):
    key = jax.random.fold_in(key, 11)
    rising = 1.0 + 2.0 * jnp.arange(POINTS, dtype=jnp.float32) / POINTS
    values = jax.random.normal(key, (PROBES, POINTS), jnp.float32) * rising[None, :]
    return jnp.clip(values, -12.0, 12.0)


def block_scale(rng, extent, pieces, smallest, high):
    level = 1.0
    for dim, blocks in pieces:
        heights = jax.random.uniform(jax.random.fold_in(jax.random.fold_in(rng, 6), dim), (blocks,), jnp.float32, smallest / len(pieces), high / len(pieces))
        level = level * jnp.repeat(jnp.exp(heights), extent[dim] // blocks).reshape((-1,) + (1,) * (len(extent) - 1 - dim))
    return level


def scatter_about(own_key, dims, scale, limit, shards=(), kind=jnp.bfloat16):
    array = jax.random.normal(own_key, dims, jnp.float32) * scale
    if len(shards) > 0:
        array = block_scale(own_key, dims, shards, -0.22, 0.18) * array
    return jnp.clip(array, min=-limit, max=limit).astype(kind)


def setup_inputs(seed: int = 0) -> dict:
    seeds = jax.random.split(jax.random.key(seed), 8)
    return {
        "features": scatter_about(seeds[0], (COMPS, FEAT, POINTS), 1.0, 6.0, ((0, 8), (2, 64)), jnp.float32),
        "lengthscale": jnp.clip(jnp.exp(math.log(3.0) - 1.0986123 * jax.random.uniform(seeds[1], (COMPS, FEAT), jnp.float32) ** block_scale(seeds[1], (COMPS, FEAT), ((0, 8),), -0.2, 0.2)), 1.0, 3.0),
        "amplitude": jnp.clip(jnp.exp(math.log(2.0) - 1.3862944 * jax.random.uniform(seeds[2], (COMPS,), jnp.float32) ** block_scale(seeds[2], (COMPS,), ((0, 8),), -0.2, 0.2)), 0.5, 2.0),
        "noise": jnp.clip(jnp.exp(jax.random.uniform(seeds[3], (1,), jnp.float32, math.log(0.5), math.log(2.0))), 0.5, 2.0),
        "solution": scatter_about(seeds[4], (PROBES, POINTS), 1.0, 6.0, ((1, 64),), jnp.float32),
        "residual": draw_residual(jax.random.fold_in(seeds[7], 71), 0),
        "direction": scatter_about(seeds[6], (PROBES, POINTS), 1.0, 6.0, ((1, 64),), jnp.float32),
    }


def reference(features, lengthscale, amplitude, noise, solution, residual, direction):
    scaled = (features / lengthscale[:, :, None]).astype(jnp.bfloat16).astype(jnp.float32)
    sq = jnp.sum(scaled * scaled, axis=1)
    dir_low = direction.astype(jnp.bfloat16).astype(jnp.float32)
    block = min(POINTS, 512)
    count = POINTS // block

    def one_block(index):
        begin = (index * block).astype(jnp.int32)
        total = jnp.zeros((PROBES, block), jnp.float32)
        for comp_id in range(COMPS):
            mine = lax.dynamic_slice_in_dim(scaled[comp_id], begin, block, 1)
            sq_mine = lax.dynamic_slice_in_dim(sq[comp_id], begin, block, 0)
            cross = jnp.dot(scaled[comp_id].T, mine, precision=lax.Precision.HIGHEST)
            dist = sq[comp_id][:, None] + sq_mine[None, :] - 2.0 * cross
            weight = (amplitude[comp_id] * jnp.exp(-0.5 * dist)).astype(jnp.bfloat16).astype(jnp.float32)
            total = total + jnp.dot(dir_low, weight, precision=lax.Precision.HIGHEST)
        return total

    blocks = lax.map(one_block, jnp.arange(count, dtype=jnp.int32))
    image = jnp.transpose(blocks, (1, 0, 2)).reshape(PROBES, POINTS) + noise[0] * direction
    norm_now = jnp.sum(residual * residual, axis=1)
    curve = jnp.sum(direction * image, axis=1)
    alpha = norm_now / curve
    new_solution = solution + alpha[:, None] * direction
    new_residual = residual - alpha[:, None] * image
    fresh = jnp.sum(new_residual * new_residual, axis=1)
    new_direction = new_residual + (fresh / norm_now)[:, None] * direction
    return new_solution, new_residual, new_direction
```

```python
import jax
import jax.numpy as jnp
from jax import lax
from jax.experimental import pallas as pl
from jax.experimental.pallas import tpu as pltpu
from jax.sharding import Mesh, PartitionSpec as P

COMPS = 8
FEAT = 16
PROBES = 128
OWN = 512
SUB = OWN // COMPS
BLOCK = 1024
NAMES = ("x", "h", "z", "y", "k")
SIZES = (4, 2, 8, 4, 2)

bf16 = jnp.bfloat16
f32 = jnp.float32


def split3(value):
    first = value.astype(bf16)
    rest = value - first.astype(f32)
    second = rest.astype(bf16)
    rest = rest - second.astype(f32)
    return first, second, rest.astype(bf16)


def dot(a, b):
    return jnp.dot(a, b, preferred_element_type=f32)


def weights_kernel(far_ref, own_ref, out_ref, lhs, dirs, rhs):
    points = far_ref.shape[0] * SUB
    lane = lax.broadcasted_iota(jnp.int32, (128, 128), 1)
    row = lax.broadcasted_iota(jnp.int32, (128, 128), 0)
    group = jnp.where((row // FEAT == lane % 8) & (lane < 24), 1.0, 0.0).astype(bf16)
    spot = lax.broadcasted_iota(jnp.int32, (256, 128), 1)

    @pl.loop(0, points // 256)
    def _(index):
        piece = far_ref[pl.ds(index * 4, 4)]
        far_dirs = piece[:, 0].reshape(256, 128)
        feats = piece[:, 1].reshape(256, 128)
        wide = feats.astype(f32)
        square = wide * wide
        high = square.astype(bf16)
        low = (square - high.astype(f32)).astype(bf16)
        half = -0.5 * (dot(high, group) + dot(low, group))
        a0, a1, a2 = (term.astype(f32) for term in split3(half))
        aux = jnp.where(spot < 8, a0, jnp.where(spot < 16, a1, jnp.where(spot < 24, a2, jnp.where(spot < 27, 1.0, 0.0))))
        rows = pl.ds(pl.multiple_of(index * 256, 256), 256)
        lhs[rows, :128] = feats
        lhs[rows, 128:] = aux.astype(bf16)
        dirs[:, rows] = far_dirs.T

    own = own_ref[...]
    feats = own[:, :, :OWN].reshape(128, OWN).astype(f32)
    line = lax.broadcasted_iota(jnp.int32, (128, OWN), 0)
    for c in range(COMPS):
        mine = own[c, :, :OWN].astype(f32)
        log_amp = jnp.sum(own[c, :, OWN:].astype(f32), axis=0, keepdims=True)[:, :1]
        offset = log_amp - 0.5 * jnp.sum(mine * mine, axis=0, keepdims=True)
        b0, b1, b2 = (jnp.broadcast_to(term.astype(f32), (128, OWN)) for term in split3(offset))
        rhs[c, :128] = jnp.where(line // FEAT == c, feats, 0.0).astype(bf16)
        tail = jnp.where(line == 24, b0, jnp.where(line == 25, b1, jnp.where(line == 26, b2, 0.0)))
        rhs[c, 128:] = jnp.where((line < 24) & (line % 8 == c), 1.0, tail).astype(bf16)

    out_ref[...] = jnp.zeros_like(out_ref)

    @pl.loop(0, points // BLOCK)
    def _(index):
        rows = pl.ds(pl.multiple_of(index * BLOCK, BLOCK), BLOCK)
        left = lhs[rows, :]
        far_dirs = dirs[:, rows]
        total = jnp.zeros((PROBES, OWN), f32)
        for c in range(COMPS):
            weight = jnp.exp(dot(left, rhs[c])).astype(bf16)
            total = total + dot(far_dirs, weight)
        out_ref[...] += total


def kernel_terms(far, own):
    points = far.shape[0] * SUB
    return pl.pallas_call(
        weights_kernel,
        out_shape=jax.ShapeDtypeStruct((PROBES, OWN), f32),
        in_specs=[pl.BlockSpec(memory_space=pltpu.VMEM)] * 2,
        out_specs=pl.BlockSpec(memory_space=pltpu.VMEM),
        scratch_shapes=[
            pltpu.VMEM((points, 256), bf16),
            pltpu.VMEM((PROBES, points), bf16),
            pltpu.VMEM((COMPS, 256, OWN), bf16),
        ],
        compiler_params=pltpu.CompilerParams(vmem_limit_bytes=48 << 20),
        cost_estimate=pl.CostEstimate(
            flops=2 * points * OWN * COMPS * 384,
            bytes_accessed=points * 512,
            transcendentals=points * OWN * COMPS,
        ),
    )(far, own)


def spread(value, axes, count):
    return lax.all_to_all(jnp.broadcast_to(value[None], (count,) + value.shape), axes, 0, 0, tiled=True)


def local(features, lengthscale, amplitude, noise, solution, residual, direction):
    comp = lax.axis_index("x") * 2 + lax.axis_index("h")
    scaled = (features[0] / lengthscale[0][:, None]).astype(bf16)
    log_amp = split3(jnp.log(amplitude))
    extra = jnp.concatenate(log_amp + (jnp.zeros((FEAT - 3,), bf16),))
    extra = jnp.broadcast_to(extra[:, None], (FEAT, 128))
    own = spread(jnp.concatenate((scaled, extra), axis=1), ("x", "h"), COMPS)

    feats = own[:, :, :OWN].reshape(COMPS * FEAT, OWN)
    both = jnp.stack((direction.astype(bf16).T, feats.T))
    piece = lax.dynamic_slice_in_dim(both, comp * SUB, SUB, 1)
    far = spread(piece, ("z", "y"), 32)
    far = lax.all_gather(far, "k", axis=0, tiled=True)

    part = kernel_terms(far, own)
    parts = spread(part.astype(bf16), ("x", "h"), COMPS)
    image = jnp.sum(parts.astype(f32), axis=0) + noise[0] * direction

    sums = jnp.stack(
        (
            jnp.sum(residual * residual, axis=1),
            jnp.sum(direction * image, axis=1),
            jnp.sum(residual * image, axis=1),
            jnp.sum(image * image, axis=1),
        )
    )
    sums = jnp.sum(spread(sums, ("z", "y", "k"), 64), axis=0)
    norm_now, curve, mixed, image_norm = sums[0], sums[1], sums[2], sums[3]
    alpha = norm_now / curve
    fresh = jnp.maximum(norm_now + alpha * (alpha * image_norm - 2.0 * mixed), 0.0)
    beta = fresh / norm_now
    new_solution = solution + alpha[:, None] * direction
    new_residual = residual - alpha[:, None] * image
    new_direction = new_residual + beta[:, None] * direction
    return new_solution, new_residual, new_direction


def solution(mesh):
    fine = Mesh(mesh.devices.reshape(SIZES), NAMES)
    comp, row = ("x", "h"), ("z", "y", "k")
    in_specs = (
        P(comp, None, row),
        P(comp, None),
        P(comp),
        P(),
        P(None, row),
        P(None, row),
        P(None, row),
    )
    out_specs = (P(None, row), P(None, row), P(None, row))
    return jax.shard_map(local, mesh=fine, in_specs=in_specs, out_specs=out_specs, check_vma=False)
```

```python
import jax
import jax.numpy as jnp
from jax import lax
from jax.experimental import pallas as pl
from jax.experimental.pallas import tpu as pltpu
from jax.sharding import Mesh, PartitionSpec as P

COMPS = 8
FEAT = 16
PROBES = 128
OWN = 512
SUB = OWN // COMPS
BLOCK = 1024
NAMES = ("x", "h", "z", "y", "k")
SIZES = (4, 2, 8, 4, 2)
PLANE = SIZES[2] * SIZES[3]
ROWS = PLANE * SIZES[4]

bf16 = jnp.bfloat16
f32 = jnp.float32
VMEM = pl.BlockSpec(memory_space=pltpu.VMEM)
SMEM = pl.BlockSpec(memory_space=pltpu.SMEM)


def split3(value):
    first = value.astype(bf16)
    rest = value - first.astype(f32)
    second = rest.astype(bf16)
    rest = rest - second.astype(f32)
    return first, second, rest.astype(bf16)


def dot(a, b):
    return jnp.dot(a, b, preferred_element_type=f32)


def call(kernel, outs, in_specs, args, scratch=(), cost=None):
    return pl.pallas_call(
        kernel,
        out_shape=tuple(jax.ShapeDtypeStruct(shape, dtype) for shape, dtype in outs),
        in_specs=in_specs,
        out_specs=(VMEM,) * len(outs),
        scratch_shapes=scratch,
        compiler_params=pltpu.CompilerParams(vmem_limit_bytes=40 << 20),
        cost_estimate=cost,
    )(*args)


def scale_kernel(features_ref, length_ref, amplitude_ref, out_ref, features, length, amplitude, sems):
    copies = [
        pltpu.make_async_copy(features_ref, features, sems.at[0]),
        pltpu.make_async_copy(length_ref, length, sems.at[1]),
        pltpu.make_async_copy(amplitude_ref, amplitude, sems.at[2]),
    ]
    for copy in copies:
        copy.start()
    for copy in copies:
        copy.wait()
    eye = lax.broadcasted_iota(jnp.int32, (FEAT, FEAT), 0) == lax.broadcasted_iota(jnp.int32, (FEAT, FEAT), 1)
    wide = jnp.sum(jnp.where(eye, length[...], 0.0), axis=1, keepdims=True)
    scaled = (features[0] / wide).astype(bf16)
    a0, a1, a2 = (term.astype(f32) for term in split3(jnp.log(jnp.full((FEAT, 128), amplitude[0], f32))))
    row = lax.broadcasted_iota(jnp.int32, (FEAT, 128), 0)
    extra = jnp.where(row == 0, a0, jnp.where(row == 1, a1, jnp.where(row == 2, a2, 0.0))).astype(bf16)
    for c in range(COMPS):
        out_ref[c, :, :OWN] = scaled
        out_ref[c, :, OWN:] = extra


def passing_kernel(begin_ref, own_ref, out_ref, turned):
    turned[...] = own_ref[:, :, :OWN].reshape(COMPS * FEAT, OWN).T
    piece = turned[pl.ds(pl.multiple_of(begin_ref[0], SUB), SUB), :]
    for index in range(PLANE):
        out_ref[index] = piece


def weights_kernel(far_ref, own_ref, mate_ref, dir_ref, mate_dir_ref, out_ref, lhs, dirs, rhs):
    line = lax.broadcasted_iota(jnp.int32, (128, OWN), 0)
    for side, (ref, side_dirs) in enumerate(((own_ref, dir_ref), (mate_ref, mate_dir_ref))):
        near = ref[...]
        columns = slice(side * OWN, (side + 1) * OWN)
        dirs[columns, :] = side_dirs[...].T
        feats = near[:, :, :OWN].reshape(128, OWN).astype(f32)
        for c in range(COMPS):
            mine = near[c, :, :OWN].astype(f32)
            log_amp = jnp.sum(near[c, :, OWN:].astype(f32), axis=0, keepdims=True)[:, :1]
            offset = log_amp - 0.5 * jnp.sum(mine * mine, axis=0, keepdims=True)
            b0, b1, b2 = (jnp.broadcast_to(term.astype(f32), (128, OWN)) for term in split3(offset))
            rhs[c, :128, columns] = jnp.where(line // FEAT == c, feats, 0.0).astype(bf16)
            tail = jnp.where(line == 24, b0, jnp.where(line == 25, b1, jnp.where(line == 26, b2, 0.0)))
            rhs[c, 128:, columns] = jnp.where((line < 24) & (line % 8 == c), 1.0, tail).astype(bf16)

    blocks = far_ref.shape[0]
    lane = lax.broadcasted_iota(jnp.int32, (128, 128), 1)
    row = lax.broadcasted_iota(jnp.int32, (128, 128), 0)
    group = jnp.where((row // FEAT == lane % 8) & (lane < 24), 1.0, 0.0).astype(bf16)
    spot = lax.broadcasted_iota(jnp.int32, (256, 128), 1)

    @pl.loop(0, blocks // 4)
    def _(index):
        feats = far_ref[pl.ds(index * 4, 4)].reshape(256, 128)
        wide = feats.astype(f32)
        square = wide * wide
        high = square.astype(bf16)
        low = (square - high.astype(f32)).astype(bf16)
        half = -0.5 * (dot(high, group) + dot(low, group))
        a0, a1, a2 = (term.astype(f32) for term in split3(half))
        aux = jnp.where(spot < 8, a0, jnp.where(spot < 16, a1, jnp.where(spot < 24, a2, jnp.where(spot < 27, 1.0, 0.0))))
        rows = pl.ds(pl.multiple_of(index * 256, 256), 256)
        lhs[rows, :128] = feats
        lhs[rows, 128:] = aux.astype(bf16)

    step = BLOCK // SUB
    for index in range(blocks // step):
        left = lhs[index * BLOCK : (index + 1) * BLOCK, :]
        weight = None
        for c in range(COMPS):
            term = jnp.exp(dot(left, rhs[c]))
            weight = term if weight is None else weight + term
        part = dot(weight.astype(bf16), dirs[...]).astype(bf16)
        out_ref[index * step : (index + 1) * step] = part.reshape(step, SUB, PROBES)


def add_kernel(parts_ref, out_ref):
    total = parts_ref[0].astype(f32)
    for index in range(1, PLANE):
        total = total + parts_ref[index].astype(f32)
    total = total.astype(bf16)
    for c in range(COMPS):
        out_ref[c] = total


def image_kernel(noise_ref, parts_ref, direction_ref, residual_ref, image_ref, sums_ref):
    direction = direction_ref[...]
    residual = residual_ref[...]
    image = parts_ref[...].reshape(OWN, PROBES).astype(f32).T + noise_ref[0] * direction
    image_ref[...] = image
    terms = (residual * residual, direction * image, residual * image, image * image)
    lane = lax.broadcasted_iota(jnp.int32, (PROBES, 8), 1)
    sums = jnp.zeros((PROBES, 8), f32)
    for index, term in enumerate(terms):
        sums = jnp.where(lane == index, jnp.sum(term, axis=1, keepdims=True), sums)
    sums = sums.T[:4]
    for index in range(ROWS):
        sums_ref[index] = sums


def update_kernel(sums_ref, image_ref, solution_ref, residual_ref, direction_ref, outs_ref, outr_ref, outd_ref):
    sums = sums_ref[0]
    for index in range(1, ROWS):
        sums = sums + sums_ref[index]
    norm_now, curve, mixed, image_norm = (sums[index : index + 1] for index in range(4))
    alpha = norm_now / curve
    fresh = jnp.maximum(norm_now + alpha * (alpha * image_norm - 2.0 * mixed), 0.0)
    beta = fresh / norm_now
    line = lax.broadcasted_iota(jnp.int32, (8, PROBES), 0)
    scalars = jnp.where(line == 0, alpha, jnp.where(line == 1, beta, 0.0)).T
    alpha, beta = scalars[:, :1], scalars[:, 1:2]
    direction = direction_ref[...]
    outs_ref[...] = solution_ref[...] + alpha * direction
    new_residual = residual_ref[...] - alpha * image_ref[...]
    outr_ref[...] = new_residual
    outd_ref[...] = new_residual + beta * direction


def swap(value):
    return lax.ppermute(value, "k", ((0, 1), (1, 0)))


def exchange(value, axes):
    return lax.all_to_all(value, axes, 0, 0, tiled=True)


def local(features, lengthscale, amplitude, noise, solution, residual, direction):
    low = direction.astype(bf16)
    mate_low = swap(low)
    (own,) = call(
        scale_kernel,
        (((COMPS, FEAT, OWN + 128), bf16),),
        (pl.BlockSpec(memory_space=pltpu.HBM),) * 3,
        (features, lengthscale, amplitude),
        (
            pltpu.VMEM((1, FEAT, OWN), f32),
            pltpu.VMEM((1, FEAT), f32),
            pltpu.SMEM((1,), f32),
            pltpu.SemaphoreType.DMA((3,)),
        ),
    )
    own = exchange(own, ("x", "h"))
    mate = swap(own)

    begin = ((lax.axis_index("x") * 2 + lax.axis_index("h")) * SUB).astype(jnp.int32)[None]
    far_shape = ((PLANE, SUB, PROBES), bf16)
    (far,) = call(passing_kernel, (far_shape,), (SMEM, VMEM), (begin, own), (pltpu.VMEM((OWN, COMPS * FEAT), bf16),))
    far = exchange(far, ("z", "y"))
    points = PLANE * SUB
    (part,) = call(
        weights_kernel,
        (far_shape,),
        (VMEM,) * 5,
        (far, own, mate, low, mate_low),
        (
            pltpu.VMEM((points, 256), bf16),
            pltpu.VMEM((2 * OWN, PROBES), bf16),
            pltpu.VMEM((COMPS, 256, 2 * OWN), bf16),
        ),
        pl.CostEstimate(
            flops=4 * points * OWN * (COMPS * 256 + 128), bytes_accessed=2 << 20, transcendentals=2 * points * OWN * COMPS
        ),
    )
    (part,) = call(add_kernel, (((COMPS, SUB, PROBES), bf16),), (VMEM,), (exchange(part, ("z", "y")),))
    image, sums = call(
        image_kernel,
        (((PROBES, OWN), f32), ((ROWS, 4, PROBES), f32)),
        (SMEM, VMEM, VMEM, VMEM),
        (noise, exchange(part, ("x", "h")), direction, residual),
    )
    sums = exchange(sums, ("z", "y", "k"))

    block = pl.BlockSpec((PROBES, OWN), lambda: (0, 0))
    return pl.pallas_call(
        update_kernel,
        out_shape=(jax.ShapeDtypeStruct((PROBES, OWN), f32),) * 3,
        in_specs=(VMEM,) * 5,
        out_specs=(block,) * 3,
        compiler_params=pltpu.CompilerParams(vmem_limit_bytes=40 << 20),
    )(sums, image, solution, residual, direction)


def solution(mesh):
    fine = Mesh(mesh.devices.reshape(SIZES), NAMES)
    comp, row = ("x", "h"), ("z", "y", "k")
    in_specs = (
        P(comp, None, row),
        P(comp, None),
        P(comp),
        P(),
        P(None, row),
        P(None, row),
        P(None, row),
    )
    out_specs = (P(None, row), P(None, row), P(None, row))
    return jax.shard_map(local, mesh=fine, in_specs=in_specs, out_specs=out_specs, check_vma=False)
```

```python
import jax
import jax.numpy as jnp
from jax import lax
from jax.experimental import pallas as pl
from jax.experimental.pallas import tpu as pltpu
from jax.sharding import Mesh, PartitionSpec as P

COMPS = 8
FEAT = 16
PROBES = 128
OWN = 512
SUB = OWN // COMPS
HALF = SUB // 2
BLOCK = 512
NAMES = ("x", "h", "u", "e", "y", "k")
SIZES = (4, 2, 4, 2, 4, 2)
COMP = ("x", "h")
PAIR = ("x", "h", "e")
CHIPS = ("u", "e", "y")
ROW = ("u", "e", "y", "k")
PLANE = 32
PARITY = tuple(tuple(i for i in range(PLANE) if i // 4 % 2 == e) for e in range(2))
ROWS = 64

bf16 = jnp.bfloat16
f32 = jnp.float32
VMEM = pl.BlockSpec(memory_space=pltpu.VMEM)
SMEM = pl.BlockSpec(memory_space=pltpu.SMEM)


def split3(value):
    first = value.astype(bf16)
    rest = value - first.astype(f32)
    second = rest.astype(bf16)
    rest = rest - second.astype(f32)
    return first, second, rest.astype(bf16)


def dot(a, b):
    return jnp.dot(a, b, preferred_element_type=f32)


def call(kernel, outs, in_specs, args, scratch=(), cost=None):
    return pl.pallas_call(
        kernel,
        out_shape=tuple(jax.ShapeDtypeStruct(shape, dtype) for shape, dtype in outs),
        in_specs=in_specs,
        out_specs=(VMEM,) * len(outs),
        scratch_shapes=scratch,
        compiler_params=pltpu.CompilerParams(vmem_limit_bytes=40 << 20),
        cost_estimate=cost,
    )(*args)


def scale_kernel(features_ref, length_ref, amplitude_ref, out_ref, features, length, amplitude, sems):
    copies = [
        pltpu.make_async_copy(features_ref, features, sems.at[0]),
        pltpu.make_async_copy(length_ref, length, sems.at[1]),
        pltpu.make_async_copy(amplitude_ref, amplitude, sems.at[2]),
    ]
    for copy in copies:
        copy.start()
    for copy in copies:
        copy.wait()
    eye = lax.broadcasted_iota(jnp.int32, (FEAT, FEAT), 0) == lax.broadcasted_iota(jnp.int32, (FEAT, FEAT), 1)
    wide = jnp.sum(jnp.where(eye, length[...], 0.0), axis=1, keepdims=True)
    scaled = (features[0] / wide).astype(bf16)
    a0, a1, a2 = (term.astype(f32) for term in split3(jnp.log(jnp.full((FEAT, 128), amplitude[0], f32))))
    row = lax.broadcasted_iota(jnp.int32, (FEAT, 128), 0)
    extra = jnp.where(row == 0, a0, jnp.where(row == 1, a1, jnp.where(row == 2, a2, 0.0))).astype(bf16)
    for index in range(2 * COMPS):
        out_ref[index, :, :OWN] = scaled
        out_ref[index, :, OWN:] = extra


def passing_kernel(place_ref, own_ref, out_ref, turned):
    columns = pl.ds(pl.multiple_of(place_ref[0] * 128, 128), 128)
    turned[...] = jnp.concatenate([own_ref[2 * c + place_ref[2], :, columns] for c in range(COMPS)]).T
    for side in range(2):
        piece = turned[pl.ds(pl.multiple_of(place_ref[1] * SUB + side * HALF, HALF), HALF), :]
        for index in PARITY[side]:
            out_ref[index] = piece


def weights_kernel(place_ref, far_ref, own_ref, mate_ref, dir_ref, mate_dir_ref, out_ref, lhs, dirs, rhs):
    parity = place_ref[2]
    for side in range(4):
        ref, side_dirs, odd = (own_ref, mate_ref)[side // 2], (dir_ref, mate_dir_ref)[side // 2], side % 2
        columns = slice(side * OWN, (side + 1) * OWN)
        dirs[columns, :] = side_dirs[parity if odd == 0 else 1 - parity].T
        for group in range(2):
            feats = jnp.concatenate([ref[2 * c + odd, :, :OWN] for c in range(4 * group, 4 * group + 4)])
            rhs[group, group * 64 : group * 64 + 64, columns] = feats
            offsets = []
            for c in range(4 * group, 4 * group + 4):
                near = ref[2 * c + odd].astype(f32)
                mine = near[:, :OWN]
                log_amp = jnp.sum(near[:, OWN:], axis=0, keepdims=True)[:, :1]
                offsets.append(log_amp - 0.5 * jnp.sum(mine * mine, axis=0, keepdims=True))
            terms = [term.astype(f32) for term in split3(jnp.concatenate(offsets))]
            tail = jnp.concatenate([jnp.ones((12, OWN), f32)] + terms + [jnp.zeros((40, OWN), f32)])
            rhs[group, 64 - group * 64 : 128 - group * 64, columns] = tail.astype(bf16)

    lane = lax.broadcasted_iota(jnp.int32, (256, 128), 1)
    spot = lane % 64
    upper = lane >= 64
    comp = lax.broadcasted_iota(jnp.int32, (128, 128), 0) // FEAT
    column = lax.broadcasted_iota(jnp.int32, (128, 128), 1)
    place = (comp % 4 == column % 4) & (column % 64 < 12) & ((comp < 4) == (column >= 64))
    place = jnp.where(place, -0.5, 0.0).astype(bf16)
    place = jnp.concatenate((place, place))
    for index in range(PLANE // 8):
        feats = far_ref[index * 8 : (index + 1) * 8].reshape(256, 128)
        wide = feats.astype(f32)
        square = wide * wide
        high = square.astype(bf16)
        low = (square - high.astype(f32)).astype(bf16)
        half = dot(jnp.concatenate((high, low), axis=1), place)
        a0, a1, a2 = (term.astype(f32) for term in split3(half))
        aux = jnp.where(spot < 8, jnp.where(spot < 4, a0, a1), jnp.where(spot < 12, a2, jnp.where(spot < 24, 1.0, 0.0)))
        rows = slice(index * 256, (index + 1) * 256)
        for c in range(COMPS):
            in_feats = upper if c >= 4 else jnp.logical_not(upper)
            keep = jnp.where(in_feats, spot // FEAT, spot % 4) == c % 4
            lhs[c, rows] = jnp.where(keep, jnp.where(in_feats, wide, aux), 0.0).astype(bf16)

    total = None
    for begin in range(0, 4 * OWN, BLOCK):
        columns = slice(begin, begin + BLOCK)
        weight = None
        for c in range(COMPS):
            term = jnp.exp(dot(lhs[c], rhs[c // 4, :, columns]))
            weight = term if weight is None else weight + term
        part = dot(weight.astype(bf16), dirs[columns, :])
        total = part if total is None else total + part
    out_ref[...] = total.astype(bf16).reshape(PLANE, HALF, PROBES)


def add_kernel(parts_ref, out_ref):
    for side in range(2):
        total = parts_ref[PARITY[side][0]].astype(f32)
        for index in PARITY[side][1:]:
            total = total + parts_ref[index].astype(f32)
        total = total.astype(bf16)
        for c in range(COMPS):
            out_ref[c, side * HALF : (side + 1) * HALF] = total


def image_kernel(noise_ref, parts_ref, direction_ref, residual_ref, image_ref, sums_ref):
    direction = direction_ref[...]
    residual = residual_ref[...]
    image = parts_ref[...].reshape(OWN, PROBES).astype(f32).T + noise_ref[0] * direction
    image_ref[...] = image
    terms = (residual * residual, direction * image, residual * image, image * image)
    lane = lax.broadcasted_iota(jnp.int32, (PROBES, 8), 1)
    sums = jnp.zeros((PROBES, 8), f32)
    for index, term in enumerate(terms):
        sums = jnp.where(lane == index, jnp.sum(term, axis=1, keepdims=True), sums)
    sums = sums.T[:4]
    for index in range(ROWS):
        sums_ref[index] = sums


def update_kernel(sums_ref, image_ref, solution_ref, residual_ref, direction_ref, outs_ref, outr_ref, outd_ref):
    sums = sums_ref[0]
    for index in range(1, ROWS):
        sums = sums + sums_ref[index]
    norm_now, curve, mixed, image_norm = (sums[index : index + 1] for index in range(4))
    alpha = norm_now / curve
    fresh = jnp.maximum(norm_now + alpha * (alpha * image_norm - 2.0 * mixed), 0.0)
    beta = fresh / norm_now
    line = lax.broadcasted_iota(jnp.int32, (8, PROBES), 0)
    scalars = jnp.where(line == 0, alpha, jnp.where(line == 1, beta, 0.0)).T
    alpha, beta = scalars[:, :1], scalars[:, 1:2]
    direction = direction_ref[...]
    outs_ref[...] = solution_ref[...] + alpha * direction
    new_residual = residual_ref[...] - alpha * image_ref[...]
    outr_ref[...] = new_residual
    outd_ref[...] = new_residual + beta * direction


def swap(value):
    return lax.ppermute(value, "k", ((0, 1), (1, 0)))


def exchange(value, axes):
    return lax.all_to_all(value, axes, 0, 0, tiled=True)


def local(features, lengthscale, amplitude, noise, solution, residual, direction):
    low = direction.astype(bf16)
    lows = jnp.stack((low, lax.ppermute(low, "e", ((0, 1), (1, 0)))))
    mate_lows = swap(lows)
    (own,) = call(
        scale_kernel,
        (((2 * COMPS, FEAT, OWN + 128), bf16),),
        (pl.BlockSpec(memory_space=pltpu.HBM),) * 3,
        (features, lengthscale, amplitude),
        (
            pltpu.VMEM((1, FEAT, OWN), f32),
            pltpu.VMEM((1, FEAT), f32),
            pltpu.SMEM((1,), f32),
            pltpu.SemaphoreType.DMA((3,)),
        ),
    )
    own = exchange(own, PAIR)
    mate = swap(own)

    place = jnp.stack([lax.axis_index(name) for name in ("x", "h", "e")]).astype(jnp.int32)
    far_shape = ((PLANE, HALF, PROBES), bf16)
    (far,) = call(passing_kernel, (far_shape,), (SMEM, VMEM), (place, own), (pltpu.VMEM((128, COMPS * FEAT), bf16),))
    far = exchange(far, CHIPS)
    points = PLANE * HALF
    (part,) = call(
        weights_kernel,
        (far_shape,),
        (SMEM,) + (VMEM,) * 5,
        (place, far, own, mate, lows, mate_lows),
        (
            pltpu.VMEM((COMPS, points, 128), bf16),
            pltpu.VMEM((4 * OWN, PROBES), bf16),
            pltpu.VMEM((2, 128, 4 * OWN), bf16),
        ),
        pl.CostEstimate(
            flops=8 * points * OWN * (COMPS * 256 + 128), bytes_accessed=2 << 20, transcendentals=4 * points * OWN * COMPS
        ),
    )
    (part,) = call(add_kernel, (((COMPS, SUB, PROBES), bf16),), (VMEM,), (exchange(part, CHIPS),))
    image, sums = call(
        image_kernel,
        (((PROBES, OWN), f32), ((ROWS, 4, PROBES), f32)),
        (SMEM, VMEM, VMEM, VMEM),
        (noise, exchange(part, COMP), direction, residual),
    )
    sums = exchange(sums, ROW)

    block = pl.BlockSpec((PROBES, OWN), lambda: (0, 0))
    return pl.pallas_call(
        update_kernel,
        out_shape=(jax.ShapeDtypeStruct((PROBES, OWN), f32),) * 3,
        in_specs=(VMEM,) * 5,
        out_specs=(block,) * 3,
        compiler_params=pltpu.CompilerParams(vmem_limit_bytes=40 << 20),
    )(sums, image, solution, residual, direction)


def solution(mesh):
    fine = Mesh(mesh.devices.reshape(SIZES), NAMES)
    comp, row = COMP, ROW
    in_specs = (
        P(comp, None, row),
        P(comp, None),
        P(comp),
        P(),
        P(None, row),
        P(None, row),
        P(None, row),
    )
    out_specs = (P(None, row), P(None, row), P(None, row))
    return jax.shard_map(local, mesh=fine, in_specs=in_specs, out_specs=out_specs, check_vma=False)
```

```python
import jax
import jax.numpy as jnp
from jax import lax
from jax.experimental import pallas as pl
from jax.experimental.pallas import tpu as pltpu
from jax.sharding import Mesh, PartitionSpec as P

COMPS = 8
FEAT = 16
PROBES = 128
OWN = 512
MINE = 4
SUB = OWN // MINE
HALF = SUB // 2
BLOCK = 1024
ROW_BLOCK = 1024
NAMES = ("x", "h", "u", "e", "y", "k")
SIZES = (4, 2, 4, 2, 4, 2)
COMP = ("x", "h")
PAIR = ("x", "e")
CHIPS = ("u", "e", "y")
ROW = ("u", "e", "y", "k")
PLANE = 32
PARITY = tuple(tuple(i for i in range(PLANE) if i // 4 % 2 == e) for e in range(2))
ROWS = 64

bf16 = jnp.bfloat16
f32 = jnp.float32
VMEM = pl.BlockSpec(memory_space=pltpu.VMEM)
SMEM = pl.BlockSpec(memory_space=pltpu.SMEM)


def split3(value):
    first = value.astype(bf16)
    rest = value - first.astype(f32)
    second = rest.astype(bf16)
    rest = rest - second.astype(f32)
    return first, second, rest.astype(bf16)


def dot(a, b):
    return jnp.dot(a, b, preferred_element_type=f32)


def call(kernel, outs, in_specs, args, scratch=(), cost=None):
    return pl.pallas_call(
        kernel,
        out_shape=tuple(jax.ShapeDtypeStruct(shape, dtype) for shape, dtype in outs),
        in_specs=in_specs,
        out_specs=(VMEM,) * len(outs),
        scratch_shapes=scratch,
        compiler_params=pltpu.CompilerParams(vmem_limit_bytes=24 << 20),
        cost_estimate=cost,
    )(*args)


def scale_kernel(features_ref, length_ref, amplitude_ref, out_ref, features, length, amplitude, sems):
    copies = [
        pltpu.make_async_copy(features_ref, features, sems.at[0]),
        pltpu.make_async_copy(length_ref, length, sems.at[1]),
        pltpu.make_async_copy(amplitude_ref, amplitude, sems.at[2]),
    ]
    for copy in copies:
        copy.start()
    for copy in copies:
        copy.wait()
    eye = lax.broadcasted_iota(jnp.int32, (FEAT, FEAT), 0) == lax.broadcasted_iota(jnp.int32, (FEAT, FEAT), 1)
    wide = jnp.sum(jnp.where(eye, length[...], 0.0), axis=1, keepdims=True)
    scaled = (features[0] / wide).astype(bf16)
    a0, a1, a2 = (term.astype(f32) for term in split3(jnp.log(jnp.full((FEAT, 128), amplitude[0], f32))))
    row = lax.broadcasted_iota(jnp.int32, (FEAT, 128), 0)
    extra = jnp.where(row == 0, a0, jnp.where(row == 1, a1, jnp.where(row == 2, a2, 0.0))).astype(bf16)
    for index in range(2 * MINE):
        out_ref[index, :, :OWN] = scaled
        out_ref[index, :, OWN:] = extra


def passing_kernel(place_ref, own_ref, out_ref):
    columns = pl.ds(pl.multiple_of(place_ref[0] * SUB, SUB), SUB)
    feats = jnp.concatenate([own_ref[2 * c + place_ref[1], :, columns] for c in range(MINE)]).astype(f32)
    turned = jnp.concatenate((feats, pltpu.roll(feats, SUB - HALF // 2, 1))).T.astype(bf16)
    for side in range(2):
        piece = turned[side * HALF : side * HALF + HALF // 2]
        for index in PARITY[side]:
            out_ref[index] = piece


def near_kernel(place_ref, own_ref, mate_ref, dir_ref, mate_dir_ref, lhs_ref, dirs_ref):
    parity = place_ref[1]
    for side in range(4):
        ref, side_dirs, odd = (own_ref, mate_ref)[side // 2], (dir_ref, mate_dir_ref)[side // 2], side % 2
        points = slice(side * OWN, (side + 1) * OWN)
        dirs_ref[:, points] = side_dirs[parity if odd == 0 else 1 - parity]
        near = [ref[2 * c + odd].astype(f32) for c in range(MINE)]
        offsets = []
        for part in near:
            mine = part[:, :OWN]
            log_amp = jnp.sum(part[:, OWN:], axis=0, keepdims=True)[:, :1]
            offsets.append(log_amp - 0.5 * jnp.sum(mine * mine, axis=0, keepdims=True))
        terms = [term.astype(f32) for term in split3(jnp.concatenate(offsets))]
        rows = [part[:, :OWN] for part in near] + [jnp.ones((12, OWN), f32)] + terms + [jnp.zeros((40, OWN), f32)]
        lhs_ref[points, :] = jnp.concatenate(rows).T.astype(bf16)


def weights_kernel(far_ref, lhs, dirs, out_ref, rhs):
    line = lax.broadcasted_iota(jnp.int32, (64, 256), 0)
    for index in range(PLANE // 4):
        turned = far_ref[index * 4 : (index + 1) * 4].reshape(128, 128).astype(f32).T
        wide = jnp.concatenate((turned[:64], turned[64:]), axis=1)
        square = wide * wide
        half = [-0.5 * jnp.sum(square[c * FEAT : (c + 1) * FEAT], axis=0, keepdims=True) for c in range(MINE)]
        terms = [term.astype(f32) for term in split3(jnp.concatenate(half))]
        tail = jnp.concatenate(terms + [jnp.ones((12, 256), f32), jnp.zeros((40, 256), f32)])
        columns = slice(index * 256, (index + 1) * 256)
        for c in range(MINE):
            rhs[c, :64, columns] = jnp.where(line // FEAT == c, wide, 0.0).astype(bf16)
            rhs[c, 64:, columns] = jnp.where(line % 4 == c, tail, 0.0).astype(bf16)

    for begin in range(0, PLANE * HALF, BLOCK):
        columns = slice(begin, begin + BLOCK)
        total = None
        for top in range(0, 4 * OWN, ROW_BLOCK):
            rows = slice(top, top + ROW_BLOCK)
            weight = None
            for c in range(MINE):
                term = jnp.exp(dot(lhs[rows, :], rhs[c, :, columns]))
                weight = term if weight is None else weight + term
            part = dot(dirs[:, rows], weight.astype(bf16))
            total = part if total is None else total + part
        for index in range(begin // 256, (begin + BLOCK) // 256):
            shift = index * 256 - begin
            for side in range(2):
                piece = total[:, shift + side * 128 : shift + side * 128 + 128].T.astype(bf16).reshape(4, HALF // 2, PROBES)
                out_ref[index * 4 : (index + 1) * 4, side * (HALF // 2) : (side + 1) * (HALF // 2)] = piece


def add_kernel(parts_ref, out_ref):
    for side in range(2):
        total = parts_ref[PARITY[side][0]].astype(f32)
        for index in PARITY[side][1:]:
            total = total + parts_ref[index].astype(f32)
        total = total.astype(bf16)
        for c in range(COMPS):
            out_ref[c, side * HALF : (side + 1) * HALF] = total


def image_kernel(noise_ref, parts_ref, direction_ref, residual_ref, image_ref, sums_ref):
    direction = direction_ref[...]
    residual = residual_ref[...]
    parts = [parts_ref[2 * x].astype(f32) + parts_ref[2 * x + 1].astype(f32) for x in range(MINE)]
    image = jnp.concatenate(parts).T + noise_ref[0] * direction
    image_ref[...] = image
    terms = (residual * residual, direction * image, residual * image, image * image)
    lane = lax.broadcasted_iota(jnp.int32, (PROBES, 8), 1)
    sums = jnp.zeros((PROBES, 8), f32)
    for index, term in enumerate(terms):
        sums = jnp.where(lane == index, jnp.sum(term, axis=1, keepdims=True), sums)
    sums = sums.T[:4]
    for index in range(ROWS):
        sums_ref[index] = sums


def update_kernel(sums_ref, image_ref, solution_ref, residual_ref, direction_ref, outs_ref, outr_ref, outd_ref):
    sums = sums_ref[0]
    for index in range(1, ROWS):
        sums = sums + sums_ref[index]
    norm_now, curve, mixed, image_norm = (sums[index : index + 1] for index in range(4))
    alpha = norm_now / curve
    fresh = jnp.maximum(norm_now + alpha * (alpha * image_norm - 2.0 * mixed), 0.0)
    beta = fresh / norm_now
    line = lax.broadcasted_iota(jnp.int32, (8, PROBES), 0)
    scalars = jnp.where(line == 0, alpha, jnp.where(line == 1, beta, 0.0)).T
    alpha, beta = scalars[:, :1], scalars[:, 1:2]
    direction = direction_ref[...]
    outs_ref[...] = solution_ref[...] + alpha * direction
    new_residual = residual_ref[...] - alpha * image_ref[...]
    outr_ref[...] = new_residual
    outd_ref[...] = new_residual + beta * direction


def swap(value):
    return lax.ppermute(value, "k", ((0, 1), (1, 0)))


def exchange(value, axes):
    return lax.all_to_all(value, axes, 0, 0, tiled=True)


def local(features, lengthscale, amplitude, noise, solution, residual, direction):
    low = direction.astype(bf16)
    lows = jnp.stack((low, lax.ppermute(low, "e", ((0, 1), (1, 0)))))
    mate_lows = swap(lows)
    (own,) = call(
        scale_kernel,
        (((2 * MINE, FEAT, OWN + 128), bf16),),
        (pl.BlockSpec(memory_space=pltpu.HBM),) * 3,
        (features, lengthscale, amplitude),
        (
            pltpu.VMEM((1, FEAT, OWN), f32),
            pltpu.VMEM((1, FEAT), f32),
            pltpu.SMEM((1,), f32),
            pltpu.SemaphoreType.DMA((3,)),
        ),
    )
    own = exchange(own, PAIR)
    mate = swap(own)

    place = jnp.stack([lax.axis_index(name) for name in ("x", "e")]).astype(jnp.int32)
    (far,) = call(passing_kernel, (((PLANE, HALF // 2, 128), bf16),), (SMEM, VMEM), (place, own))
    far = exchange(far, CHIPS)
    points = PLANE * HALF
    near, dirs = call(
        near_kernel,
        (((4 * OWN, 128), bf16), ((PROBES, 4 * OWN), bf16)),
        (SMEM,) + (VMEM,) * 4,
        (place, own, mate, lows, mate_lows),
        cost=pl.CostEstimate(flops=1 << 20, bytes_accessed=2 << 20, transcendentals=0),
    )
    (part,) = call(
        weights_kernel,
        (((PLANE, HALF, PROBES), bf16),),
        (VMEM,) * 3,
        (far, near, dirs),
        (pltpu.VMEM((MINE, 128, points), bf16),),
        pl.CostEstimate(
            flops=8 * points * OWN * (MINE * 256 + 128), bytes_accessed=2 << 20, transcendentals=4 * points * OWN * MINE
        ),
    )
    (part,) = call(add_kernel, (((COMPS, SUB, PROBES), bf16),), (VMEM,), (exchange(part, CHIPS),))
    image, sums = call(
        image_kernel,
        (((PROBES, OWN), f32), ((ROWS, 4, PROBES), f32)),
        (SMEM, VMEM, VMEM, VMEM),
        (noise, exchange(part, COMP), direction, residual),
    )
    sums = exchange(sums, ROW)

    block = pl.BlockSpec((PROBES, OWN), lambda: (0, 0))
    return pl.pallas_call(
        update_kernel,
        out_shape=(jax.ShapeDtypeStruct((PROBES, OWN), f32),) * 3,
        in_specs=(VMEM,) * 5,
        out_specs=(block,) * 3,
        compiler_params=pltpu.CompilerParams(vmem_limit_bytes=24 << 20),
    )(sums, image, solution, residual, direction)


def solution(mesh):
    fine = Mesh(mesh.devices.reshape(SIZES), NAMES)
    comp, row = COMP, ROW
    in_specs = (
        P(comp, None, row),
        P(comp, None),
        P(comp),
        P(),
        P(None, row),
        P(None, row),
        P(None, row),
    )
    out_specs = (P(None, row), P(None, row), P(None, row))
    return jax.shard_map(local, mesh=fine, in_specs=in_specs, out_specs=out_specs, check_vma=False)
```

```python
import jax
import jax.numpy as jnp
from jax import lax
from jax.experimental import pallas as pl
from jax.experimental.pallas import tpu as pltpu
from jax.sharding import Mesh, PartitionSpec as P

COMPS = 8
FEAT = 16
PROBES = 128
OWN = 512
MINE = 4
SUB = OWN // MINE
LEAP = SUB // 2
BLOCK = 1024
ROW_BLOCK = 1024
NAMES = ("x", "h", "z", "w", "e", "k")
SIZES = (4, 2, 8, 2, 2, 2)
COMP = ("x", "h")
PAIR = ("x", "e")
CHIPS = ("z", "w")
ROW = ("z", "w", "e", "k")
FAR = 16
ROWS = 64

bf16 = jnp.bfloat16
f32 = jnp.float32
VMEM = pl.BlockSpec(memory_space=pltpu.VMEM)
SMEM = pl.BlockSpec(memory_space=pltpu.SMEM)


def split3(value):
    first = value.astype(bf16)
    rest = value - first.astype(f32)
    second = rest.astype(bf16)
    rest = rest - second.astype(f32)
    return first, second, rest.astype(bf16)


def dot(a, b):
    return jnp.dot(a, b, preferred_element_type=f32)


def call(kernel, outs, in_specs, args, scratch=(), cost=None, vmem=24 << 20):
    return pl.pallas_call(
        kernel,
        out_shape=tuple(jax.ShapeDtypeStruct(shape, dtype) for shape, dtype in outs),
        in_specs=in_specs,
        out_specs=(VMEM,) * len(outs),
        scratch_shapes=scratch,
        compiler_params=pltpu.CompilerParams(vmem_limit_bytes=vmem),
        cost_estimate=cost,
    )(*args)


def scale_kernel(features_ref, length_ref, amplitude_ref, out_ref, features, length, amplitude, sems):
    copies = [
        pltpu.make_async_copy(features_ref, features, sems.at[0]),
        pltpu.make_async_copy(length_ref, length, sems.at[1]),
        pltpu.make_async_copy(amplitude_ref, amplitude, sems.at[2]),
    ]
    for copy in copies:
        copy.start()
    for copy in copies:
        copy.wait()
    eye = lax.broadcasted_iota(jnp.int32, (FEAT, FEAT), 0) == lax.broadcasted_iota(jnp.int32, (FEAT, FEAT), 1)
    wide = jnp.sum(jnp.where(eye, length[...], 0.0), axis=1, keepdims=True)
    scaled = (features[0] / wide).astype(bf16)
    a0, a1, a2 = (term.astype(f32) for term in split3(jnp.log(jnp.full((FEAT, 128), amplitude[0], f32))))
    row = lax.broadcasted_iota(jnp.int32, (FEAT, 128), 0)
    extra = jnp.where(row == 0, a0, jnp.where(row == 1, a1, jnp.where(row == 2, a2, 0.0))).astype(bf16)
    for index in range(2 * MINE):
        out_ref[index, :, :OWN] = scaled
        out_ref[index, :, OWN:] = extra


def passing_kernel(own_ref, out_ref):
    parity = lax.axis_index("e")
    columns = pl.ds(pl.multiple_of(lax.axis_index("x") * SUB, SUB), SUB)
    feats = jnp.concatenate([own_ref[2 * c + parity, :, columns] for c in range(MINE)]).astype(f32)
    turned = jnp.concatenate((feats, pltpu.roll(feats, LEAP, 1))).T.astype(bf16)
    for index in range(FAR):
        out_ref[index] = turned[:LEAP]


def near_kernel(own_ref, mate_ref, dir_ref, mate_dir_ref, lhs_ref, dirs_ref):
    parity = lax.axis_index("e")
    for side in range(4):
        ref, side_dirs, odd = (own_ref, mate_ref)[side // 2], (dir_ref, mate_dir_ref)[side // 2], side % 2
        points = slice(side * OWN, (side + 1) * OWN)
        dirs_ref[:, points] = side_dirs[parity if odd == 0 else 1 - parity]
        near = [ref[2 * c + odd].astype(f32) for c in range(MINE)]
        offsets = []
        for part in near:
            mine = part[:, :OWN]
            log_amp = jnp.sum(part[:, OWN:], axis=0, keepdims=True)[:, :1]
            offsets.append(log_amp - 0.5 * jnp.sum(mine * mine, axis=0, keepdims=True))
        terms = [term.astype(f32) for term in split3(jnp.concatenate(offsets))]
        rows = [part[:, :OWN] for part in near] + [jnp.ones((12, OWN), f32)] + terms + [jnp.zeros((40, OWN), f32)]
        lhs_ref[points, :] = jnp.concatenate(rows).T.astype(bf16)


def weights_kernel(far_ref, lhs, dirs, out_ref, rhs):
    line = lax.broadcasted_iota(jnp.int32, (64, 256), 0)
    for index in range(FAR // 2):
        turned = far_ref[index * 2 : (index + 1) * 2].reshape(128, 128).astype(f32).T
        wide = jnp.concatenate((turned[:64], turned[64:]), axis=1)
        square = wide * wide
        half = [-0.5 * jnp.sum(square[c * FEAT : (c + 1) * FEAT], axis=0, keepdims=True) for c in range(MINE)]
        terms = [term.astype(f32) for term in split3(jnp.concatenate(half))]
        tail = jnp.concatenate(terms + [jnp.ones((12, 256), f32), jnp.zeros((40, 256), f32)])
        columns = slice(index * 256, (index + 1) * 256)
        for c in range(MINE):
            rhs[c, :64, columns] = jnp.where(line // FEAT == c, wide, 0.0).astype(bf16)
            rhs[c, 64:, columns] = jnp.where(line % 4 == c, tail, 0.0).astype(bf16)

    for begin in range(0, FAR * SUB, BLOCK):
        columns = slice(begin, begin + BLOCK)
        total = None
        for top in range(0, 4 * OWN, ROW_BLOCK):
            rows = slice(top, top + ROW_BLOCK)
            weight = None
            for c in range(MINE):
                term = jnp.exp(dot(lhs[rows, :], rhs[c, :, columns]))
                weight = term if weight is None else weight + term
            part = dot(dirs[:, rows], weight.astype(bf16))
            total = part if total is None else total + part
        for index in range(begin // 256, (begin + BLOCK) // 256):
            shift = index * 256 - begin
            for side in range(2):
                piece = total[:, shift + side * 128 : shift + side * 128 + 128].T.astype(bf16).reshape(2, LEAP, PROBES)
                out_ref[index * 2 : (index + 1) * 2, side * LEAP : (side + 1) * LEAP] = piece


def add_kernel(parts_ref, out_ref):
    total = parts_ref[0].astype(f32)
    for index in range(1, FAR):
        total = total + parts_ref[index].astype(f32)
    total = total.astype(bf16)
    for c in range(COMPS):
        out_ref[c] = total


def image_kernel(noise_ref, parts_ref, direction_ref, residual_ref, image_ref, sums_ref):
    direction = direction_ref[...]
    residual = residual_ref[...]
    parts = [parts_ref[2 * x].astype(f32) + parts_ref[2 * x + 1].astype(f32) for x in range(MINE)]
    image = jnp.concatenate(parts).T + noise_ref[0] * direction
    image_ref[...] = image
    terms = (residual * residual, direction * image, residual * image, image * image)
    lane = lax.broadcasted_iota(jnp.int32, (PROBES, 8), 1)
    sums = jnp.zeros((PROBES, 8), f32)
    for index, term in enumerate(terms):
        sums = jnp.where(lane == index, jnp.sum(term, axis=1, keepdims=True), sums)
    sums = sums.T[:4]
    for index in range(ROWS):
        sums_ref[index] = sums


def update_kernel(sums_ref, image_ref, solution_ref, residual_ref, direction_ref, outs_ref, outr_ref, outd_ref):
    sums = sums_ref[0]
    for index in range(1, ROWS):
        sums = sums + sums_ref[index]
    norm_now, curve, mixed, image_norm = (sums[index : index + 1] for index in range(4))
    alpha = norm_now / curve
    fresh = jnp.maximum(norm_now + alpha * (alpha * image_norm - 2.0 * mixed), 0.0)
    beta = fresh / norm_now
    line = lax.broadcasted_iota(jnp.int32, (8, PROBES), 0)
    scalars = jnp.where(line == 0, alpha, jnp.where(line == 1, beta, 0.0)).T
    alpha, beta = scalars[:, :1], scalars[:, 1:2]
    direction = direction_ref[...]
    outs_ref[...] = solution_ref[...] + alpha * direction
    new_residual = residual_ref[...] - alpha * image_ref[...]
    outr_ref[...] = new_residual
    outd_ref[...] = new_residual + beta * direction


def swap(value):
    return lax.ppermute(value, "k", ((0, 1), (1, 0)))


def exchange(value, axes):
    return lax.all_to_all(value, axes, 0, 0, tiled=True)


def local(features, lengthscale, amplitude, noise, solution, residual, direction):
    low = direction.astype(bf16)
    lows = jnp.stack((low, lax.ppermute(low, "e", ((0, 1), (1, 0)))))
    mate_lows = swap(lows)
    (own,) = call(
        scale_kernel,
        (((2 * MINE, FEAT, OWN + 128), bf16),),
        (pl.BlockSpec(memory_space=pltpu.HBM),) * 3,
        (features, lengthscale, amplitude),
        (
            pltpu.VMEM((1, FEAT, OWN), f32),
            pltpu.VMEM((1, FEAT), f32),
            pltpu.SMEM((1,), f32),
            pltpu.SemaphoreType.DMA((3,)),
        ),
        vmem=60 << 20,
    )
    own = exchange(own, PAIR)
    mate = swap(own)

    (far,) = call(passing_kernel, (((FAR, LEAP, 128), bf16),), (VMEM,), (own,))
    far = exchange(far, CHIPS)
    points = FAR * SUB
    near, dirs = call(
        near_kernel,
        (((4 * OWN, 128), bf16), ((PROBES, 4 * OWN), bf16)),
        (VMEM,) * 4,
        (own, mate, lows, mate_lows),
        cost=pl.CostEstimate(flops=1 << 20, bytes_accessed=2 << 20, transcendentals=0),
    )
    (part,) = call(
        weights_kernel,
        (((FAR, SUB, PROBES), bf16),),
        (VMEM,) * 3,
        (far, near, dirs),
        (pltpu.VMEM((MINE, 128, points), bf16),),
        pl.CostEstimate(
            flops=8 * points * OWN * (MINE * 256 + 128), bytes_accessed=2 << 20, transcendentals=4 * points * OWN * MINE
        ),
    )
    (part,) = call(add_kernel, (((COMPS, SUB, PROBES), bf16),), (VMEM,), (exchange(part, CHIPS),))
    image, sums = call(
        image_kernel,
        (((PROBES, OWN), f32), ((ROWS, 4, PROBES), f32)),
        (SMEM, VMEM, VMEM, VMEM),
        (noise, exchange(part, COMP), direction, residual),
    )
    sums = exchange(sums, ROW)

    block = pl.BlockSpec((PROBES, OWN), lambda: (0, 0))
    return pl.pallas_call(
        update_kernel,
        out_shape=(jax.ShapeDtypeStruct((PROBES, OWN), f32),) * 3,
        in_specs=(VMEM,) * 5,
        out_specs=(block,) * 3,
        compiler_params=pltpu.CompilerParams(vmem_limit_bytes=24 << 20),
    )(sums, image, solution, residual, direction)


def solution(mesh):
    fine = Mesh(mesh.devices.reshape(SIZES), NAMES)
    comp, row = COMP, ROW
    in_specs = (
        P(comp, None, row),
        P(comp, None),
        P(comp),
        P(),
        P(None, row),
        P(None, row),
        P(None, row),
    )
    out_specs = (P(None, row), P(None, row), P(None, row))
    return jax.shard_map(local, mesh=fine, in_specs=in_specs, out_specs=out_specs, check_vma=False)
```

```python
import jax
import jax.numpy as jnp
from jax import lax
from jax.experimental import pallas as pl
from jax.experimental.pallas import tpu as pltpu
from jax.sharding import Mesh, PartitionSpec as P

COMPS = 8
FEAT = 16
PROBES = 128
OWN = 512
MINE = 4
SUB = OWN // MINE
LEAP = SUB // 2
BLOCK = 1024
ROW_BLOCK = 1024
NAMES = ("x", "h", "z", "w", "e", "k")
SIZES = (4, 2, 8, 2, 2, 2)
COMP = ("x", "h")
PAIR = ("x", "e")
CHIPS = ("z", "w")
ROW = ("z", "w", "e", "k")
FAR = 16
ROWS = 64

bf16 = jnp.bfloat16
f32 = jnp.float32
VMEM = pl.BlockSpec(memory_space=pltpu.VMEM)
SMEM = pl.BlockSpec(memory_space=pltpu.SMEM)


def split3(value):
    first = value.astype(bf16)
    rest = value - first.astype(f32)
    second = rest.astype(bf16)
    rest = rest - second.astype(f32)
    return first, second, rest.astype(bf16)


def dot(a, b):
    return jnp.dot(a, b, preferred_element_type=f32)


def call(kernel, outs, in_specs, args, scratch=(), cost=None, vmem=24 << 20):
    return pl.pallas_call(
        kernel,
        out_shape=tuple(jax.ShapeDtypeStruct(shape, dtype) for shape, dtype in outs),
        in_specs=in_specs,
        out_specs=(VMEM,) * len(outs),
        scratch_shapes=scratch,
        compiler_params=pltpu.CompilerParams(vmem_limit_bytes=vmem),
        cost_estimate=cost,
    )(*args)


def scale_kernel(features_ref, length_ref, amplitude_ref, out_ref, features, length, amplitude, sems):
    copies = [
        pltpu.make_async_copy(features_ref, features, sems.at[0]),
        pltpu.make_async_copy(length_ref, length, sems.at[1]),
        pltpu.make_async_copy(amplitude_ref, amplitude, sems.at[2]),
    ]
    for copy in copies:
        copy.start()
    for copy in copies:
        copy.wait()
    eye = lax.broadcasted_iota(jnp.int32, (FEAT, FEAT), 0) == lax.broadcasted_iota(jnp.int32, (FEAT, FEAT), 1)
    wide = jnp.sum(jnp.where(eye, length[...], 0.0), axis=1, keepdims=True)
    scaled = (features[0] / wide).astype(bf16)
    a0, a1, a2 = (term.astype(f32) for term in split3(jnp.log(jnp.full((FEAT, 128), amplitude[0], f32))))
    row = lax.broadcasted_iota(jnp.int32, (FEAT, 128), 0)
    extra = jnp.where(row == 0, a0, jnp.where(row == 1, a1, jnp.where(row == 2, a2, 0.0))).astype(bf16)
    for index in range(2 * MINE):
        out_ref[index, :, :OWN] = scaled
        out_ref[index, :, OWN:] = extra


def passing_kernel(own_ref, out_ref):
    parity = lax.axis_index("e")
    columns = pl.ds(pl.multiple_of(lax.axis_index("x") * SUB, SUB), SUB)
    feats = jnp.concatenate([own_ref[2 * c + parity, :, columns] for c in range(MINE)]).astype(f32)
    turned = jnp.concatenate((feats, pltpu.roll(feats, LEAP, 1))).T.astype(bf16)
    for index in range(FAR):
        out_ref[index] = turned[:LEAP]


def near_kernel(feats_ref, dir_ref, lhs_ref, dirs_ref):
    parity = lax.axis_index("e")
    for side in range(4):
        core, odd = side // 2, side % 2
        points = slice(side * OWN, (side + 1) * OWN)
        dirs_ref[:, points] = dir_ref[2 * core + (parity if odd == 0 else 1 - parity)]
        near = [feats_ref[core, 2 * c + odd].astype(f32) for c in range(MINE)]
        offsets = []
        for part in near:
            mine = part[:, :OWN]
            log_amp = jnp.sum(part[:, OWN:], axis=0, keepdims=True)[:, :1]
            offsets.append(log_amp - 0.5 * jnp.sum(mine * mine, axis=0, keepdims=True))
        terms = [term.astype(f32) for term in split3(jnp.concatenate(offsets))]
        rows = [part[:, :OWN] for part in near] + [jnp.ones((12, OWN), f32)] + terms + [jnp.zeros((40, OWN), f32)]
        lhs_ref[points, :] = jnp.concatenate(rows).T.astype(bf16)


def weights_kernel(far_ref, lhs, dirs, out_ref, rhs):
    line = lax.broadcasted_iota(jnp.int32, (64, 256), 0)
    for index in range(FAR // 2):
        turned = far_ref[index * 2 : (index + 1) * 2].reshape(128, 128).astype(f32).T
        wide = jnp.concatenate((turned[:64], turned[64:]), axis=1)
        square = wide * wide
        half = [-0.5 * jnp.sum(square[c * FEAT : (c + 1) * FEAT], axis=0, keepdims=True) for c in range(MINE)]
        terms = [term.astype(f32) for term in split3(jnp.concatenate(half))]
        tail = jnp.concatenate(terms + [jnp.ones((12, 256), f32), jnp.zeros((40, 256), f32)])
        columns = slice(index * 256, (index + 1) * 256)
        for c in range(MINE):
            rhs[c, :64, columns] = jnp.where(line // FEAT == c, wide, 0.0).astype(bf16)
            rhs[c, 64:, columns] = jnp.where(line % 4 == c, tail, 0.0).astype(bf16)

    for begin in range(0, FAR * SUB, BLOCK):
        columns = slice(begin, begin + BLOCK)
        total = None
        for top in range(0, 4 * OWN, ROW_BLOCK):
            rows = slice(top, top + ROW_BLOCK)
            weight = None
            for c in range(MINE):
                term = jnp.exp(dot(lhs[rows, :], rhs[c, :, columns]))
                weight = term if weight is None else weight + term
            part = dot(dirs[:, rows], weight.astype(bf16))
            total = part if total is None else total + part
        for index in range(begin // 256, (begin + BLOCK) // 256):
            shift = index * 256 - begin
            for side in range(2):
                piece = total[:, shift + side * 128 : shift + side * 128 + 128].T.astype(bf16).reshape(2, LEAP, PROBES)
                out_ref[index * 2 : (index + 1) * 2, side * LEAP : (side + 1) * LEAP] = piece


def add_kernel(parts_ref, out_ref):
    total = parts_ref[0].astype(f32)
    for index in range(1, FAR):
        total = total + parts_ref[index].astype(f32)
    total = total.astype(bf16)
    for c in range(COMPS):
        out_ref[c] = total


def image_kernel(noise_ref, parts_ref, direction_ref, residual_ref, image_ref, sums_ref):
    direction = direction_ref[...]
    residual = residual_ref[...]
    parts = [parts_ref[2 * x].astype(f32) + parts_ref[2 * x + 1].astype(f32) for x in range(MINE)]
    image = jnp.concatenate(parts).T + noise_ref[0] * direction
    image_ref[...] = image
    terms = (residual * residual, direction * image, residual * image, image * image)
    lane = lax.broadcasted_iota(jnp.int32, (PROBES, 8), 1)
    sums = jnp.zeros((PROBES, 8), f32)
    for index, term in enumerate(terms):
        sums = jnp.where(lane == index, jnp.sum(term, axis=1, keepdims=True), sums)
    sums = sums.T[:4]
    for index in range(ROWS):
        sums_ref[index] = sums


def update_kernel(sums_ref, image_ref, solution_ref, residual_ref, direction_ref, outs_ref, outr_ref, outd_ref):
    sums = sums_ref[0]
    for index in range(1, ROWS):
        sums = sums + sums_ref[index]
    norm_now, curve, mixed, image_norm = (sums[index : index + 1] for index in range(4))
    alpha = norm_now / curve
    fresh = jnp.maximum(norm_now + alpha * (alpha * image_norm - 2.0 * mixed), 0.0)
    beta = fresh / norm_now
    line = lax.broadcasted_iota(jnp.int32, (8, PROBES), 0)
    scalars = jnp.where(line == 0, alpha, jnp.where(line == 1, beta, 0.0)).T
    alpha, beta = scalars[:, :1], scalars[:, 1:2]
    direction = direction_ref[...]
    outs_ref[...] = solution_ref[...] + alpha * direction
    new_residual = residual_ref[...] - alpha * image_ref[...]
    outr_ref[...] = new_residual
    outd_ref[...] = new_residual + beta * direction


def exchange(value, axes):
    return lax.all_to_all(value, axes, 0, 0, tiled=True)


def local(features, lengthscale, amplitude, noise, solution, residual, direction):
    low = direction.astype(bf16)
    lows = jnp.stack((low, lax.ppermute(low, "e", ((0, 1), (1, 0)))))
    lows = lax.all_gather(lows, "k", axis=0, tiled=True)
    (own,) = call(
        scale_kernel,
        (((2 * MINE, FEAT, OWN + 128), bf16),),
        (pl.BlockSpec(memory_space=pltpu.HBM),) * 3,
        (features, lengthscale, amplitude),
        (
            pltpu.VMEM((1, FEAT, OWN), f32),
            pltpu.VMEM((1, FEAT), f32),
            pltpu.SMEM((1,), f32),
            pltpu.SemaphoreType.DMA((3,)),
        ),
        vmem=60 << 20,
    )
    own = exchange(own, PAIR)
    feats = lax.all_gather(own, "k")

    (far,) = call(passing_kernel, (((FAR, LEAP, 128), bf16),), (VMEM,), (own,))
    far = exchange(far, CHIPS)
    points = FAR * SUB
    near, dirs = call(
        near_kernel,
        (((4 * OWN, 128), bf16), ((PROBES, 4 * OWN), bf16)),
        (VMEM,) * 2,
        (feats, lows),
        cost=pl.CostEstimate(flops=1 << 20, bytes_accessed=2 << 20, transcendentals=0),
    )
    (part,) = call(
        weights_kernel,
        (((FAR, SUB, PROBES), bf16),),
        (VMEM,) * 3,
        (far, near, dirs),
        (pltpu.VMEM((MINE, 128, points), bf16),),
        pl.CostEstimate(
            flops=8 * points * OWN * (MINE * 256 + 128), bytes_accessed=2 << 20, transcendentals=4 * points * OWN * MINE
        ),
    )
    (part,) = call(add_kernel, (((COMPS, SUB, PROBES), bf16),), (VMEM,), (exchange(part, CHIPS),))
    image, sums = call(
        image_kernel,
        (((PROBES, OWN), f32), ((ROWS, 4, PROBES), f32)),
        (SMEM, VMEM, VMEM, VMEM),
        (noise, exchange(part, COMP), direction, residual),
    )
    sums = exchange(sums, ROW)

    block = pl.BlockSpec((PROBES, OWN), lambda: (0, 0))
    return pl.pallas_call(
        update_kernel,
        out_shape=(jax.ShapeDtypeStruct((PROBES, OWN), f32),) * 3,
        in_specs=(VMEM,) * 5,
        out_specs=(block,) * 3,
        compiler_params=pltpu.CompilerParams(vmem_limit_bytes=24 << 20),
    )(sums, image, solution, residual, direction)


def solution(mesh):
    fine = Mesh(mesh.devices.reshape(SIZES), NAMES)
    comp, row = COMP, ROW
    in_specs = (
        P(comp, None, row),
        P(comp, None),
        P(comp),
        P(),
        P(None, row),
        P(None, row),
        P(None, row),
    )
    out_specs = (P(None, row), P(None, row), P(None, row))
    return jax.shard_map(local, mesh=fine, in_specs=in_specs, out_specs=out_specs, check_vma=False)
```

```python
import jax
import jax.numpy as jnp
from jax import lax
from jax.experimental import pallas as pl
from jax.experimental.pallas import tpu as pltpu
from jax.sharding import Mesh, PartitionSpec as P

COMPS = 8
FEAT = 16
PROBES = 128
OWN = 512
MINE = 4
SUB = OWN // MINE
LEAP = SUB // 2
BLOCK = 1024
ROW_BLOCK = 2048
NAMES = ("x", "h", "z", "w", "e", "k")
SIZES = (4, 2, 8, 2, 2, 2)
COMP = ("x", "h")
PAIR = ("x", "e")
CHIPS = ("z", "w")
ROW = ("z", "w", "e", "k")
FAR = 16
ROWS = 64

bf16 = jnp.bfloat16
f32 = jnp.float32
VMEM = pl.BlockSpec(memory_space=pltpu.VMEM)
SMEM = pl.BlockSpec(memory_space=pltpu.SMEM)


def split3(value):
    first = value.astype(bf16)
    rest = value - first.astype(f32)
    second = rest.astype(bf16)
    rest = rest - second.astype(f32)
    return first, second, rest.astype(bf16)


def dot(a, b):
    return jnp.dot(a, b, preferred_element_type=f32)


def call(kernel, outs, in_specs, args, scratch=(), cost=None, vmem=24 << 20):
    return pl.pallas_call(
        kernel,
        out_shape=tuple(jax.ShapeDtypeStruct(shape, dtype) for shape, dtype in outs),
        in_specs=in_specs,
        out_specs=(VMEM,) * len(outs),
        scratch_shapes=scratch,
        compiler_params=pltpu.CompilerParams(vmem_limit_bytes=vmem),
        cost_estimate=cost,
    )(*args)


def scale_kernel(features_ref, length_ref, amplitude_ref, out_ref, features, length, amplitude, sems):
    copies = [
        pltpu.make_async_copy(features_ref, features, sems.at[0]),
        pltpu.make_async_copy(length_ref, length, sems.at[1]),
        pltpu.make_async_copy(amplitude_ref, amplitude, sems.at[2]),
    ]
    for copy in copies:
        copy.start()
    for copy in copies:
        copy.wait()
    eye = lax.broadcasted_iota(jnp.int32, (FEAT, FEAT), 0) == lax.broadcasted_iota(jnp.int32, (FEAT, FEAT), 1)
    wide = jnp.sum(jnp.where(eye, length[...], 0.0), axis=1, keepdims=True)
    scaled = (features[0] / wide).astype(bf16)
    a0, a1, a2 = (term.astype(f32) for term in split3(jnp.log(jnp.full((FEAT, 128), amplitude[0], f32))))
    row = lax.broadcasted_iota(jnp.int32, (FEAT, 128), 0)
    extra = jnp.where(row == 0, a0, jnp.where(row == 1, a1, jnp.where(row == 2, a2, 0.0))).astype(bf16)
    for index in range(2 * MINE):
        out_ref[index, :, :OWN] = scaled
        out_ref[index, :, OWN:] = extra


def passing_kernel(own_ref, out_ref):
    parity = lax.axis_index("e")
    columns = pl.ds(pl.multiple_of(lax.axis_index("x") * SUB, SUB), SUB)
    feats = jnp.concatenate([own_ref[2 * c + parity, :, columns] for c in range(MINE)]).astype(f32)
    turned = jnp.concatenate((feats, pltpu.roll(feats, LEAP, 1))).T.astype(bf16)
    for index in range(FAR):
        out_ref[index] = turned[:LEAP]


def near_kernel(feats_ref, dir_ref, lhs_ref, dirs_ref):
    parity = lax.axis_index("e")
    for side in range(4):
        core, odd = side // 2, side % 2
        points = slice(side * OWN, (side + 1) * OWN)
        dirs_ref[:, points] = dir_ref[2 * core + (parity if odd == 0 else 1 - parity)]
        near = [feats_ref[core, 2 * c + odd].astype(f32) for c in range(MINE)]
        offsets = []
        for part in near:
            mine = part[:, :OWN]
            log_amp = jnp.sum(part[:, OWN:], axis=0, keepdims=True)[:, :1]
            offsets.append(log_amp - 0.5 * jnp.sum(mine * mine, axis=0, keepdims=True))
        terms = [term.astype(f32) for term in split3(jnp.concatenate(offsets))]
        rows = [part[:, :OWN] for part in near] + [jnp.ones((12, OWN), f32)] + terms + [jnp.zeros((40, OWN), f32)]
        lhs_ref[points, :] = jnp.concatenate(rows).T.astype(bf16)


def weights_kernel(far_ref, lhs, dirs, out_ref, rhs):
    line = lax.broadcasted_iota(jnp.int32, (64, 256), 0)
    for index in range(FAR // 2):
        turned = far_ref[index * 2 : (index + 1) * 2].reshape(128, 128).astype(f32).T
        wide = jnp.concatenate((turned[:64], turned[64:]), axis=1)
        square = wide * wide
        half = [-0.5 * jnp.sum(square[c * FEAT : (c + 1) * FEAT], axis=0, keepdims=True) for c in range(MINE)]
        terms = [term.astype(f32) for term in split3(jnp.concatenate(half))]
        tail = jnp.concatenate(terms + [jnp.ones((12, 256), f32), jnp.zeros((40, 256), f32)])
        columns = slice(index * 256, (index + 1) * 256)
        for c in range(MINE):
            rhs[c, :64, columns] = jnp.where(line // FEAT == c, wide, 0.0).astype(bf16)
            rhs[c, 64:, columns] = jnp.where(line % 4 == c, tail, 0.0).astype(bf16)

    for begin in range(0, FAR * SUB, BLOCK):
        columns = slice(begin, begin + BLOCK)
        total = None
        for top in range(0, 4 * OWN, ROW_BLOCK):
            rows = slice(top, top + ROW_BLOCK)
            weight = None
            for c in range(MINE):
                term = jnp.exp(dot(lhs[rows, :], rhs[c, :, columns]))
                weight = term if weight is None else weight + term
            part = dot(dirs[:, rows], weight.astype(bf16))
            total = part if total is None else total + part
        for index in range(begin // 256, (begin + BLOCK) // 256):
            shift = index * 256 - begin
            for side in range(2):
                piece = total[:, shift + side * 128 : shift + side * 128 + 128].T.astype(bf16).reshape(2, LEAP, PROBES)
                out_ref[index * 2 : (index + 1) * 2, side * LEAP : (side + 1) * LEAP] = piece


def add_kernel(parts_ref, out_ref):
    total = parts_ref[0].astype(f32)
    for index in range(1, FAR):
        total = total + parts_ref[index].astype(f32)
    total = total.astype(bf16)
    for c in range(COMPS):
        out_ref[c] = total


def image_kernel(noise_ref, parts_ref, direction_ref, residual_ref, image_ref, sums_ref):
    direction = direction_ref[...]
    residual = residual_ref[...]
    parts = [parts_ref[2 * x].astype(f32) + parts_ref[2 * x + 1].astype(f32) for x in range(MINE)]
    image = jnp.concatenate(parts).T + noise_ref[0] * direction
    image_ref[...] = image
    terms = (residual * residual, direction * image, residual * image, image * image)
    lane = lax.broadcasted_iota(jnp.int32, (PROBES, 8), 1)
    sums = jnp.zeros((PROBES, 8), f32)
    for index, term in enumerate(terms):
        sums = jnp.where(lane == index, jnp.sum(term, axis=1, keepdims=True), sums)
    sums = sums.T[:4]
    for index in range(ROWS):
        sums_ref[index] = sums


def update_kernel(sums_ref, image_ref, solution_ref, residual_ref, direction_ref, outs_ref, outr_ref, outd_ref):
    sums = sums_ref[0]
    for index in range(1, ROWS):
        sums = sums + sums_ref[index]
    norm_now, curve, mixed, image_norm = (sums[index : index + 1] for index in range(4))
    alpha = norm_now / curve
    fresh = jnp.maximum(norm_now + alpha * (alpha * image_norm - 2.0 * mixed), 0.0)
    beta = fresh / norm_now
    line = lax.broadcasted_iota(jnp.int32, (8, PROBES), 0)
    scalars = jnp.where(line == 0, alpha, jnp.where(line == 1, beta, 0.0)).T
    alpha, beta = scalars[:, :1], scalars[:, 1:2]
    direction = direction_ref[...]
    outs_ref[...] = solution_ref[...] + alpha * direction
    new_residual = residual_ref[...] - alpha * image_ref[...]
    outr_ref[...] = new_residual
    outd_ref[...] = new_residual + beta * direction


def exchange(value, axes):
    return lax.all_to_all(value, axes, 0, 0, tiled=True)


def local(features, lengthscale, amplitude, noise, solution, residual, direction):
    low = direction.astype(bf16)
    lows = jnp.stack((low, lax.ppermute(low, "e", ((0, 1), (1, 0)))))
    lows = lax.all_gather(lows, "k", axis=0, tiled=True)
    (own,) = call(
        scale_kernel,
        (((2 * MINE, FEAT, OWN + 128), bf16),),
        (pl.BlockSpec(memory_space=pltpu.HBM),) * 3,
        (features, lengthscale, amplitude),
        (
            pltpu.VMEM((1, FEAT, OWN), f32),
            pltpu.VMEM((1, FEAT), f32),
            pltpu.SMEM((1,), f32),
            pltpu.SemaphoreType.DMA((3,)),
        ),
        vmem=60 << 20,
    )
    own = exchange(own, PAIR)
    feats = lax.all_gather(own, "k")

    (far,) = call(passing_kernel, (((FAR, LEAP, 128), bf16),), (VMEM,), (own,))
    far = exchange(far, CHIPS)
    points = FAR * SUB
    near, dirs = call(
        near_kernel,
        (((4 * OWN, 128), bf16), ((PROBES, 4 * OWN), bf16)),
        (VMEM,) * 2,
        (feats, lows),
        cost=pl.CostEstimate(flops=1 << 20, bytes_accessed=2 << 20, transcendentals=0),
    )
    (part,) = call(
        weights_kernel,
        (((FAR, SUB, PROBES), bf16),),
        (VMEM,) * 3,
        (far, near, dirs),
        (pltpu.VMEM((MINE, 128, points), bf16),),
        pl.CostEstimate(
            flops=8 * points * OWN * (MINE * 256 + 128), bytes_accessed=2 << 20, transcendentals=4 * points * OWN * MINE
        ),
    )
    (part,) = call(add_kernel, (((COMPS, SUB, PROBES), bf16),), (VMEM,), (exchange(part, CHIPS),))
    image, sums = call(
        image_kernel,
        (((PROBES, OWN), f32), ((ROWS, 4, PROBES), f32)),
        (SMEM, VMEM, VMEM, VMEM),
        (noise, exchange(part, COMP), direction, residual),
    )
    sums = exchange(sums, ROW)

    block = pl.BlockSpec((PROBES, OWN), lambda: (0, 0))
    return pl.pallas_call(
        update_kernel,
        out_shape=(jax.ShapeDtypeStruct((PROBES, OWN), f32),) * 3,
        in_specs=(VMEM,) * 5,
        out_specs=(block,) * 3,
        compiler_params=pltpu.CompilerParams(vmem_limit_bytes=24 << 20),
    )(sums, image, solution, residual, direction)


def solution(mesh):
    fine = Mesh(mesh.devices.reshape(SIZES), NAMES)
    comp, row = COMP, ROW
    in_specs = (
        P(comp, None, row),
        P(comp, None),
        P(comp),
        P(),
        P(None, row),
        P(None, row),
        P(None, row),
    )
    out_specs = (P(None, row), P(None, row), P(None, row))
    return jax.shard_map(local, mesh=fine, in_specs=in_specs, out_specs=out_specs, check_vma=False)
```
